256 devices in a mesh: row: 8 (over z), col: 32 (over y, x, core).
Axes of the slice: x: 4, y: 4, z: 8, core: 2. Of those that a mesh axis runs over, the one named last changes fastest.
Arguments:
- tokens: bfloat16 [1024, 16384], P('col', 'row'), may hold values from -6 to 6
- gate_weight: bfloat16 [16384, 28672], P('row', 'col'), may hold values from -0.0625 to 0.0625
- up_weight: bfloat16 [16384, 28672], P('row', 'col'), may hold values from -0.0625 to 0.0625
- down_weight: bfloat16 [28672, 16384], P('col', 'row'), may hold values from -0.046875 to 0.046875
- gate_mask: int32 [128, 224], P('row', 'col'), may hold values 0 or 1
- up_mask: int32 [128, 224], P('row', 'col'), may hold values 0 or 1
- down_mask: int32 [224, 128], P('col', 'row'), may hold values 0 or 1
Outputs:
- ffn_out: bfloat16 [1024, 16384], P('col', 'row')
The draws below stay inside these ranges and needn't reach their ends.
Inputs may be any that keep to these rules, and one draw needn't show every extreme that they name: `gate_mask`: 0 drops a block, 1 keeps it. `up_mask`: 0 drops a block, 1 keeps it. `down_mask`: 0 drops a block, 1 keeps it.
All inputs are finite; a program needn't handle non-finite values.
Results may differ from the reference program's by a relative error of at most 0.0049.
Values may be sent and summed in bfloat16 or wider, within the bound.
A program may use at most 128 MiB of HBM per device.

```python
import jax
import jax.numpy as jnp
from jax import lax

D = 16384
FF = 28672
BLOCK = 128
TOKENS = 1024


def touch_ends(values, own_key, least, high):
    index_at = [jax.random.randint(jax.random.fold_in(own_key, axis), (), 0, length) for axis, length in enumerate(values.shape)]
    longest = values.shape.index(max(values.shape))
    beside = index_at[:longest] + [(index_at[longest] + 1) % values.shape[longest]] + index_at[longest + 1:]
    return values.at[tuple(index_at)].set(least).at[tuple(beside)].set(high)


def block_levels(own_key, shape, cuts, low, largest):
    def one(dim, shards_of):
        steps = jax.random.uniform(jax.random.fold_in(jax.random.fold_in(own_key, 6), dim), (shards_of,), jnp.float32, low / len(cuts), largest / len(cuts))
        return jnp.repeat(jnp.exp(steps), shape[dim] // shards_of).reshape((-1,) + (1,) * (len(shape) - dim - 1))

    loudness = one(*cuts[0])
    for cut in cuts[1:]:
        loudness = loudness * one(*cut)
    return loudness


def gaussian(key, shape, spread, bound, cuts=(), kind=jnp.bfloat16):
    entries = jax.random.normal(key, shape, jnp.float32) * spread
    if len(cuts) > 0:
        entries = block_levels(key, shape, cuts, -0.22, 0.18) * entries
    return jnp.clip(entries, min=-bound, max=bound).astype(kind)


def setup_inputs(seed: int = 0) -> dict:
    keys = jax.random.split(jax.random.key(seed), 8)
    tokens = gaussian(keys[0], (TOKENS, D), 1.0, 6.0, ((0, 32), (1, 8)))
    gate_weight = gaussian(keys[1], (D, FF), (D // 2) ** -0.5, 0.0625, ((0, 8), (1, 32)))
    up_weight = gaussian(keys[2], (D, FF), (D // 2) ** -0.5, 0.0625, ((0, 8), (1, 32)))
    down_weight = gaussian(keys[3], (FF, D), (FF // 2) ** -0.5, 0.046875, ((0, 32), (1, 8)))
    gate_mask = touch_ends((jax.random.randint(keys[4], (D // BLOCK, FF // BLOCK), 0, 2) < 1).astype(jnp.int32), jax.random.fold_in(keys[4], 1), 0, 1)
    up_mask = touch_ends((jax.random.randint(keys[5], (D // BLOCK, FF // BLOCK), 0, 2) < 1).astype(jnp.int32), jax.random.fold_in(keys[5], 1), 0, 1)
    down_mask = touch_ends((jax.random.randint(keys[6], (FF // BLOCK, D // BLOCK), 0, 2) < 1).astype(jnp.int32), jax.random.fold_in(keys[6], 1), 0, 1)
    return {"tokens": tokens, "gate_weight": gate_weight, "up_weight": up_weight, "down_weight": down_weight, "gate_mask": gate_mask, "up_mask": up_mask, "down_mask": down_mask}


def keep_blocks(weight, mask):
    rows, cols = mask.shape
    full = jnp.broadcast_to(mask[:, None, :, None], (rows, BLOCK, cols, BLOCK)).reshape(rows * BLOCK, cols * BLOCK)
    return weight * full.astype(weight.dtype)


def reference(tokens, gate_weight, up_weight, down_weight, gate_mask, up_mask, down_mask):
    width = 16 * BLOCK
    count = FF // width

    def advance(total, index):
        start = (index * width).astype(jnp.int32)
        mstart = (index * 16).astype(jnp.int32)
        gate_part = keep_blocks(lax.dynamic_slice_in_dim(gate_weight, start, width, 1), lax.dynamic_slice_in_dim(gate_mask, mstart, 16, 1))
        up_part = keep_blocks(lax.dynamic_slice_in_dim(up_weight, start, width, 1), lax.dynamic_slice_in_dim(up_mask, mstart, 16, 1))
        down_part = keep_blocks(lax.dynamic_slice_in_dim(down_weight, start, width, 0), lax.dynamic_slice_in_dim(down_mask, mstart, 16, 0))
        gate = jnp.dot(tokens, gate_part, preferred_element_type=jnp.float32)
        upper = jnp.dot(tokens, up_part, preferred_element_type=jnp.float32)
        hidden = (jax.nn.silu(gate) * upper).astype(jnp.bfloat16)
        return total + jnp.dot(hidden, down_part, preferred_element_type=jnp.float32), None

    start_total = jnp.zeros((tokens.shape[0], down_weight.shape[1]), jnp.float32)
    total, _ = lax.scan(advance, start_total, jnp.arange(count, dtype=jnp.int32))
    return total.astype(jnp.bfloat16)
```

```python
import functools

import jax
import jax.numpy as jnp
from jax import lax
from jax.experimental import pallas as pl
from jax.experimental.pallas import tpu as pltpu
from jax.sharding import PartitionSpec as P

MESH = pl.DeviceIdType.MESH
BLOCK = 128
ROWS = 8
SIDE = 4
CORES = 2
CHUNKS = 8
OWN = 16
WIDTH = 256
BF16 = jnp.bfloat16
F32 = jnp.float32


def kernel(
    gate_mask, up_mask, down_mask, tokens, gate_weight, up_weight, down_weight, out,
    pair, down, tok, part, msg_out, msg_in, low_out, low_in, wide_out, wide_in,
    hid, term, sibling, out_send, out_recv,
    w_sem, tok_own, tok_send, tok_recv, fwd_send, fwd_recv,
    msg_send, msg_recv, low_send, low_recv, wide_send, wide_recv,
    ag_send, ag_recv, ex_send, ex_recv, res_send, res_recv,
):
    z = lax.axis_index("row")
    col = lax.axis_index("col")
    core = lax.rem(col, CORES)
    chip = lax.div(col, CORES)
    x = lax.rem(chip, SIDE)
    y = lax.div(chip, SIDE)
    ff = gate_weight.shape[1]
    depth = gate_weight.shape[0]
    halves = (slice(0, ff), slice(ff, 2 * ff))

    def ring(step):
        return lax.rem(z + step + ROWS, ROWS)

    def at_offset(j, sign, to_core):
        dx, dy = lax.rem(j, SIDE), lax.div(j, SIDE)
        x2 = lax.rem(x + sign * dx + SIDE, SIDE)
        y2 = lax.rem(y + sign * dy + SIDE, SIDE)
        return (z, (y2 * SIDE + x2) * CORES + to_core)

    def remote(src, dst, send, recv, device):
        return pltpu.make_async_remote_copy(
            src_ref=src, dst_ref=dst, send_sem=send, recv_sem=recv,
            device_id=device, device_id_type=MESH,
        )

    mate = (z, chip * CORES + 1 - core)
    neighbour = ((ring(1), col), (ring(-1), col))

    quarter = depth // 4
    w_copies = []
    for i in range(4):
        rows = slice(i * quarter, (i + 1) * quarter)
        for h, w in enumerate((gate_weight, up_weight)):
            w_copies.append(
                pltpu.make_async_copy(w.at[rows], pair.at[rows, halves[h]], w_sem.at[h, i])
            )
    d_copy = pltpu.make_async_copy(down_weight, down, w_sem.at[2, 0])
    own_copy = pltpu.make_async_copy(tokens, tok.at[0, 0, core], tok_own)
    own_copy.start()
    for copy in w_copies:
        copy.start()
    d_copy.start()

    barrier = pltpu.get_barrier_semaphore()
    pl.semaphore_signal(barrier, inc=1, device_id=mate, device_id_type=MESH)
    for side in range(2):
        pl.semaphore_signal(barrier, inc=1, device_id=neighbour[side], device_id_type=MESH)

    @pl.loop(1, SIDE * SIDE)
    def _(j):
        pl.semaphore_signal(barrier, inc=1, device_id=at_offset(j, 1, core), device_id_type=MESH)

    pl.semaphore_wait(barrier, SIDE * SIDE - 1 + 3)

    def tok_copy(j):
        k, p = lax.div(j, 2), lax.rem(j, 2)
        return remote(
            tokens, tok.at[k, p, core], tok_send.at[j], tok_recv.at[j], at_offset(j, -1, core)
        )

    def fwd_copy(k):
        return remote(tok.at[k, :, core], tok.at[k, :, core], fwd_send.at[k], fwd_recv.at[k], mate)

    def msg_copy(side, s, c):
        src, dst = msg_out.at[side, s, c], msg_in.at[side, s, c]
        if s == 0:
            src, dst = src.at[:, halves[side]], dst.at[:, halves[side]]
        return remote(src, dst, msg_send.at[side, s, c], msg_recv.at[side, s, c], neighbour[side])

    def low_copy(side, c):
        return remote(
            low_out.at[side, c], low_in.at[side, c],
            low_send.at[side, c], low_recv.at[side, c], neighbour[side],
        )

    def wide_copy(side, c):
        return remote(
            wide_out.at[side, c], wide_in.at[side, c],
            wide_send.at[side, c], wide_recv.at[side, c], neighbour[side],
        )

    cut = 4 * BLOCK

    def ag_ref(side, s, c, owner):
        ref = hid.at[c, owner]
        if s == 3:
            ref = ref.at[:, slice(0, cut) if side == 0 else slice(cut, ff)]
        return ref

    def ag_copy(side, s, c):
        block = ag_ref(side, s, c, ring(-s if side == 0 else s))
        return remote(block, block, ag_send.at[side, s, c], ag_recv.at[side, s, c], neighbour[side])

    def ex_copy(c):
        return remote(
            term.at[c, :, 1 - core], sibling.at[c], ex_send.at[c], ex_recv.at[c], mate
        )

    def res_copy(j):
        k, p = lax.div(j, 2), lax.rem(j, 2)
        return remote(
            out_send.at[k, p], out_recv.at[j], res_send.at[j], res_recv.at[j], at_offset(j, 1, core)
        )

    def keep(ref, rows, lanes, flag):
        scale = jnp.full((BLOCK, BLOCK), flag.astype(F32), F32).astype(BF16)
        ref[rows, lanes] = ref[rows, lanes] * scale

    def mask_pair(i):
        @pl.loop(0, quarter // BLOCK)
        def _(r):
            block = i * (quarter // BLOCK) + r
            rows = pl.ds(pl.multiple_of(block * BLOCK, BLOCK), BLOCK)
            for h, mask in enumerate((gate_mask, up_mask)):
                for b in range(ff // BLOCK):
                    start = h * ff + b * BLOCK
                    keep(pair, rows, slice(start, start + BLOCK), mask[block, b])

    def mask_down():
        @pl.loop(0, ff // BLOCK)
        def _(r):
            rows = pl.ds(pl.multiple_of(r * BLOCK, BLOCK), BLOCK)
            for b in range(down.shape[1] // BLOCK):
                keep(down, rows, slice(b * BLOCK, (b + 1) * BLOCK), down_mask[r, b])

    def first_matmul(c):
        @pl.loop(0, 2 * ff // WIDTH)
        def _(n):
            lanes = pl.ds(pl.multiple_of(n * WIDTH, WIDTH), WIDTH)
            value = jnp.dot(
                tok[c].reshape(CHUNKS * OWN, depth), pair[:, lanes], preferred_element_type=F32
            )
            part[c, :, :, lanes] = value.reshape(ROWS, OWN, WIDTH)

    def down_matmul(c):
        @pl.loop(0, down.shape[1] // WIDTH)
        def _(n):
            lanes = pl.ds(pl.multiple_of(n * WIDTH, WIDTH), WIDTH)
            value = jnp.dot(
                hid[c].reshape(ROWS * OWN, ff), down[:, lanes], preferred_element_type=F32
            )
            term[c, :, :, :, lanes] = value.reshape(2, CORES, 2 * OWN, WIDTH)

    def sum_start(c):
        owner = ring(4)
        for side in range(2):
            h = halves[side]
            msg_out[side, 0, c, :, h] = part[c, owner, :, h].astype(BF16)
            msg_copy(side, 0, c).start()

    def sum_step(s, c):
        for side in range(2):
            owner = ring(4 - s if side == 0 else s - 4)
            msg_copy(side, s - 1, c).wait_recv()
            for h in range(2):
                lanes = halves[h]
                value = part[c, owner, :, lanes]
                if s > 1 or h == side:
                    value = value + msg_in[side, s - 1, c, :, lanes].astype(F32)
                if s < 3:
                    msg_out[side, s, c, :, lanes] = value.astype(BF16)
                elif h == side:
                    wide_out[side, c] = value
                else:
                    low_out[side, c] = value.astype(BF16)
            if s < 3:
                msg_copy(side, s, c).start()
            else:
                wide_copy(side, c).start()
                low_copy(side, c).start()

    def sum_end(c):
        for side in range(2):
            wide_copy(side, c).wait_recv()
            low_copy(side, c).wait_recv()
        gate = part[c, z, :, halves[0]] + wide_in[0, c] + low_in[1, c].astype(F32)
        up = part[c, z, :, halves[1]] + wide_in[1, c] + low_in[0, c].astype(F32)
        hid[c, z] = (gate / (1.0 + jnp.exp(-gate)) * up).astype(BF16)
        for side in range(2):
            ag_copy(side, 0, c).start()

    def gather_step(s, c):
        for side in range(2):
            ag_copy(side, s - 1, c).wait_recv()
            ag_copy(side, s, c).start()

    def gather_end(c):
        for side in range(2):
            ag_copy(side, 3, c).wait_recv()
        down_matmul(c)
        ex_copy(c).start()

    def send_result(c):
        ex_copy(c).wait_recv()
        for p in range(2):
            value = term[c, p, core] + sibling[c, p]
            term[c, p, core] = value
            out_send[c, p] = value.astype(BF16)
            if p == 1:
                res_copy(2 * c + p).start()
            else:
                @pl.when(c > 0)
                def _():
                    res_copy(2 * c).start()

    tok_copy(1).start()
    for j in (2, 3):
        tok_copy(j).start()
    for i in range(4):
        w_copies[2 * i].wait()
        w_copies[2 * i + 1].wait()
        mask_pair(i)
    own_copy.wait()
    tok_copy(1).wait_recv()
    fwd_copy(0).start()

    def at(c, stage, *args):
        @pl.when(jnp.logical_and(c >= 0, c < CHUNKS))
        def _():
            stage(*args, c)

    @pl.loop(0, CHUNKS + 9)
    def _(t):
        @pl.when(t + 2 < CHUNKS)
        def _():
            tok_copy(2 * t + 4).start()
            tok_copy(2 * t + 5).start()

        for s in (3, 2, 1):
            at(t - 4 - s, gather_step, s)
        at(t - 4, sum_end)
        for s in (3, 2, 1):
            at(t - s, sum_step, s)

        @pl.when(t + 1 < CHUNKS)
        def _():
            tok_copy(2 * t + 2).wait_recv()
            tok_copy(2 * t + 3).wait_recv()
            fwd_copy(t + 1).start()

        @pl.when(t < CHUNKS)
        def _():
            fwd_copy(t).wait_recv()
            first_matmul(t)
            sum_start(t)

        @pl.when(t == 1)
        def _():
            d_copy.wait()
            mask_down()

        at(t - 9, send_result)
        at(t - 8, gather_end)


    def add(j, _):
        res_copy(j).wait_recv()
        term[0, 0, core] = term[0, 0, core] + out_recv[j].astype(F32)
        return 0

    lax.fori_loop(1, SIDE * SIDE, add, 0)
    out[...] = term[0, 0, core].astype(BF16)

    @pl.loop(0, CHUNKS)
    def _(c):
        for side in range(2):
            for s in range(3):
                msg_copy(side, s, c).wait_send()
            low_copy(side, c).wait_send()
            wide_copy(side, c).wait_send()
            for s in range(4):
                ag_copy(side, s, c).wait_send()
        fwd_copy(c).wait_send()
        ex_copy(c).wait_send()

    @pl.loop(1, SIDE * SIDE)
    def _(j):
        tok_copy(j).wait_send()
        res_copy(j).wait_send()


def body(tokens, gate_weight, up_weight, down_weight, gate_mask, up_mask, down_mask):
    depth, ff = gate_weight.shape
    wide = down_weight.shape[1]
    own_tokens = tokens.shape[0]
    dma = pltpu.SemaphoreType.DMA
    chips = SIDE * SIDE
    smem = pl.BlockSpec(memory_space=pltpu.SMEM)
    anywhere = pl.BlockSpec(memory_space=pl.ANY)
    n_tokens = own_tokens * chips * CORES
    return pl.pallas_call(
        kernel,
        out_shape=jax.ShapeDtypeStruct((own_tokens, wide), BF16),
        in_specs=[smem] * 3 + [anywhere] * 4,
        out_specs=pl.BlockSpec(memory_space=pltpu.VMEM),
        scratch_shapes=[
            pltpu.VMEM((depth, 2 * ff), BF16),
            pltpu.VMEM((ff, wide), BF16),
            pltpu.VMEM((CHUNKS, 2, CORES, own_tokens, depth), BF16),
            pltpu.VMEM((CHUNKS, ROWS, OWN, 2 * ff), F32),
            pltpu.VMEM((2, 3, CHUNKS, OWN, 2 * ff), BF16),
            pltpu.VMEM((2, 3, CHUNKS, OWN, 2 * ff), BF16),
            pltpu.VMEM((2, CHUNKS, OWN, ff), BF16),
            pltpu.VMEM((2, CHUNKS, OWN, ff), BF16),
            pltpu.VMEM((2, CHUNKS, OWN, ff), F32),
            pltpu.VMEM((2, CHUNKS, OWN, ff), F32),
            pltpu.VMEM((CHUNKS, ROWS, OWN, ff), BF16),
            pltpu.VMEM((CHUNKS, 2, CORES, own_tokens, wide), F32),
            pltpu.VMEM((CHUNKS, 2, own_tokens, wide), F32),
            pltpu.VMEM((CHUNKS, 2, own_tokens, wide), BF16),
            pltpu.VMEM((chips, own_tokens, wide), BF16),
            dma((3, 4)),
            dma,
            dma((chips,)), dma((chips,)),
            dma((CHUNKS,)), dma((CHUNKS,)),
            dma((2, 3, CHUNKS)), dma((2, 3, CHUNKS)),
            dma((2, CHUNKS)), dma((2, CHUNKS)),
            dma((2, CHUNKS)), dma((2, CHUNKS)),
            dma((2, 4, CHUNKS)), dma((2, 4, CHUNKS)),
            dma((CHUNKS,)), dma((CHUNKS,)),
            dma((chips,)), dma((chips,)),
        ],
        compiler_params=pltpu.CompilerParams(
            collective_id=0, has_side_effects=True, vmem_limit_bytes=60 * 2**20
        ),
        cost_estimate=pl.CostEstimate(
            flops=6 * n_tokens * depth * ff,
            bytes_accessed=6 * depth * ff,
            transcendentals=n_tokens * ff // ROWS,
        ),
    )(gate_mask, up_mask, down_mask, tokens, gate_weight, up_weight, down_weight)


def solution(mesh):
    placed = (
        P("col", "row"),
        P("row", "col"),
        P("row", "col"),
        P("col", "row"),
        P("row", "col"),
        P("row", "col"),
        P("col", "row"),
    )
    return jax.shard_map(
        body, mesh=mesh, in_specs=placed, out_specs=P("col", "row"), check_vma=False
    )
```

```python
import functools

import jax
import jax.numpy as jnp
from jax import lax
from jax.experimental import pallas as pl
from jax.experimental.pallas import tpu as pltpu
from jax.sharding import PartitionSpec as P

MESH = pl.DeviceIdType.MESH
BLOCK = 128
ROWS = 8
SIDE = 4
CORES = 2
CHUNKS = 8
OWN = 16
WIDTH1 = 896
WIDTH2 = 1024
GROUP = 1
AHEAD = 2
OFFSETS = (
    ((0, 0), (1, 0)),
    ((3, 0), (0, 1)),
    ((1, 1), (0, 2)),
    ((2, 1), (1, 2)),
    ((3, 2), (2, 3)),
    ((2, 2), (3, 3)),
    ((3, 1), (1, 3)),
    ((0, 3), (2, 0)),
)
OWN_PLACE = (0, 0)
WAVES = (
    (
        (0, 1, (1, 0), OWN_PLACE),
        (1, 0, (-1, 0), OWN_PLACE),
        (1, 1, (0, 1), OWN_PLACE),
        (7, 0, (0, -1), OWN_PLACE),
    ),
    (
        (2, 0, (0, 1), (0, 1)),
        (2, 1, (0, -1), (7, 0)),
        (6, 1, (1, 0), (7, 0)),
        (6, 0, (-1, 0), (1, 1)),
    ),
    (
        (3, 0, (1, 0), (2, 0)),
        (3, 1, (0, 1), (2, 0)),
        (4, 0, (-1, 0), (2, 1)),
        (4, 1, (1, 0), (6, 1)),
    ),
    (
        (5, 0, (1, 0), (3, 1)),
        (5, 1, (0, -1), (1, 0)),
        (7, 1, (-1, 0), (1, 0)),
    ),
)
DOUBLE = 1
SLOTS = CHUNKS - DOUBLE
ORDER = (
    "bring_early",
    "gather2",
    "gather1",
    "prepare_down",
    "gather_end",
    "sum_end",
    "sum3",
    "sum2",
    "sum1",
    "bring_late",
    "matmul",
    "send_result",
    "collect",
)
DX, DY = (
    tuple(sum(pair[p][i] * 4**k for k, pair in enumerate(OFFSETS)) for p in range(2))
    for i in range(2)
)


def pick(digits, k):
    return lax.rem(lax.shift_right_logical(jnp.int32(digits), jnp.int32(2 * k)), 4)

BF16 = jnp.bfloat16
F32 = jnp.float32


def kernel(
    gate_mask, up_mask, down_mask, tokens, gate_weight, up_weight, down_weight, out,
    pair, down, tok, part, msg_out, msg_in, low_out, low_in, wide_out, wide_in,
    hid, term, sibling, out_send, out_recv, acc,
    w_sem, tok_own, tok_send, tok_recv, fwd_send, fwd_recv,
    msg_send, msg_recv, low_send, low_recv, wide_send, wide_recv,
    ag_send, ag_recv, ex_send, ex_recv, res_send, res_recv,
):
    z = lax.axis_index("row")
    col = lax.axis_index("col")
    core = lax.rem(col, CORES)
    chip = lax.div(col, CORES)
    x = lax.rem(chip, SIDE)
    y = lax.div(chip, SIDE)
    ff = gate_weight.shape[1]
    depth = gate_weight.shape[0]
    halves = (slice(0, ff), slice(ff, 2 * ff))

    def ring(step):
        return lax.rem(z + step + ROWS, ROWS)

    def at_offset(k, p, sign, to_core):
        dx, dy = pick(DX[p], k), pick(DY[p], k)
        x2 = lax.rem(x + sign * dx + SIDE, SIDE)
        y2 = lax.rem(y + sign * dy + SIDE, SIDE)
        return (z, (y2 * SIDE + x2) * CORES + to_core)

    def remote(src, dst, send, recv, device):
        return pltpu.make_async_remote_copy(
            src_ref=src, dst_ref=dst, send_sem=send, recv_sem=recv,
            device_id=device, device_id_type=MESH,
        )

    mate = (z, chip * CORES + 1 - core)
    neighbour = ((ring(1), col), (ring(-1), col))
    second = ((ring(2), col), (ring(-2), col))

    quarter = depth // 4
    w_copies = []
    for i in range(4):
        rows = slice(i * quarter, (i + 1) * quarter)
        for h, w in enumerate((gate_weight, up_weight)):
            w_copies.append(
                pltpu.make_async_copy(w.at[rows], pair.at[rows, halves[h]], w_sem.at[h, i])
            )
    d_copy = pltpu.make_async_copy(down_weight, down, w_sem.at[2, 0])
    own_copy = pltpu.make_async_copy(tokens, tok.at[OWN_PLACE[0], OWN_PLACE[1], core], tok_own)
    own_copy.start()
    for copy in w_copies:
        copy.start()
    d_copy.start()

    barrier = pltpu.get_barrier_semaphore()
    pl.semaphore_signal(barrier, inc=1, device_id=mate, device_id_type=MESH)
    for side in range(2):
        pl.semaphore_signal(barrier, inc=1, device_id=neighbour[side], device_id_type=MESH)
        pl.semaphore_signal(barrier, inc=1, device_id=second[side], device_id_type=MESH)

    def others(k, p, run):
        if p == 1:
            run()
        else:
            pl.when(k > 0)(run)

    @pl.loop(0, CHUNKS)
    def _(k):
        for p in range(2):
            others(k, p, lambda: pl.semaphore_signal(
                barrier, inc=1, device_id=at_offset(k, p, 1, core), device_id_type=MESH
            ))

    pl.semaphore_wait(barrier, SIDE * SIDE - 1 + 5)

    def send_wave(number):
        for k, p, (dx, dy), (from_k, from_p) in WAVES[number]:
            x2, y2 = lax.rem(x - dx + SIDE, SIDE), lax.rem(y - dy + SIDE, SIDE)
            src = tokens if number == 0 else tok.at[from_k, from_p, core]
            remote(
                src, tok.at[k, p, core], tok_send.at[k, p], tok_recv.at[k, p],
                (z, (y2 * SIDE + x2) * CORES + core),
            ).start()

    def tok_wait(k, p):
        return remote(
            tok.at[k, p, core], tok.at[k, p, core], tok_send.at[k, p], tok_recv.at[k, p], mate
        )

    def fwd_copy(k):
        return remote(tok.at[k, :, core], tok.at[k, :, core], fwd_send.at[k], fwd_recv.at[k], mate)

    def msg_copy(side, s, c):
        src, dst = msg_out.at[side, s, c], msg_in.at[side, s, c]
        if s == 0:
            src, dst = src.at[:, halves[side]], dst.at[:, halves[side]]
        return remote(src, dst, msg_send.at[side, s, c], msg_recv.at[side, s, c], neighbour[side])

    def low_copy(side, c):
        return remote(
            low_out.at[side, c], low_in.at[side, c],
            low_send.at[side, c], low_recv.at[side, c], neighbour[side],
        )

    def wide_copy(side, c):
        return remote(
            wide_out.at[side, c], wide_in.at[side, c],
            wide_send.at[side, c], wide_recv.at[side, c], neighbour[side],
        )

    cut = 4 * BLOCK

    def ag_ref(side, s, c, owner):
        ref = hid.at[c, owner]
        if s == 3:
            ref = ref.at[:, slice(0, cut) if side == 0 else slice(cut, ff)]
        return ref

    def ag_copy(side, s, c):
        far = min(s, 2)
        block = ag_ref(side, s, c, ring(-far if side == 0 else far))
        device = second[side] if s == 3 else neighbour[side]
        return remote(block, block, ag_send.at[side, s, c], ag_recv.at[side, s, c], device)

    def ex_copy(c):
        return remote(
            term.at[c, :, 1 - core], sibling.at[c], ex_send.at[c], ex_recv.at[c], mate
        )

    def res_copy(k, p):
        return remote(
            out_send.at[k, p], out_recv.at[k, p], res_send.at[k, p], res_recv.at[k, p],
            at_offset(k, p, 1, core),
        )

    def keep(ref, rows, lanes, flag):
        scale = jnp.full((BLOCK, BLOCK), flag.astype(F32), F32).astype(BF16)
        ref[rows, lanes] = ref[rows, lanes] * scale

    def mask_pair(i):
        @pl.loop(0, quarter // BLOCK)
        def _(r):
            block = i * (quarter // BLOCK) + r
            rows = pl.ds(pl.multiple_of(block * BLOCK, BLOCK), BLOCK)
            for h, mask in enumerate((gate_mask, up_mask)):
                for b in range(ff // BLOCK):
                    start = h * ff + b * BLOCK
                    keep(pair, rows, slice(start, start + BLOCK), mask[block, b])

    def mask_down(r):
        rows = pl.ds(pl.multiple_of(r * BLOCK, BLOCK), BLOCK)
        for b in range(down.shape[1] // BLOCK):
            keep(down, rows, slice(b * BLOCK, (b + 1) * BLOCK), down_mask[r, b])

    def first_matmul(c):
        @pl.loop(0, 2 * ff // WIDTH1)
        def _(n):
            lanes = pl.ds(pl.multiple_of(n * WIDTH1, WIDTH1), WIDTH1)
            value = jnp.dot(
                tok[pl.ds(c, GROUP)].reshape(GROUP * ROWS * OWN, depth),
                pair[:, lanes],
                preferred_element_type=F32,
            )
            part[pl.ds(c, GROUP), :, :, lanes] = value.reshape(GROUP, ROWS, OWN, WIDTH1)

    def down_matmul(c):
        @pl.loop(0, down.shape[1] // WIDTH2)
        def _(n):
            lanes = pl.ds(pl.multiple_of(n * WIDTH2, WIDTH2), WIDTH2)
            value = jnp.dot(
                hid[c].reshape(ROWS * OWN, ff), down[:, lanes], preferred_element_type=F32
            )
            term[c, :, :, :, lanes] = value.reshape(2, CORES, 2 * OWN, WIDTH2)

    def sum_start(c):
        owner = ring(4)
        for side in range(2):
            h = halves[side]
            msg_out[side, 0, c, :, h] = part[c, owner, :, h].astype(BF16)
            msg_copy(side, 0, c).start()

    def sum_step(s, c):
        for side in range(2):
            owner = ring(4 - s if side == 0 else s - 4)
            msg_copy(side, s - 1, c).wait_recv()
            for h in range(2):
                lanes = halves[h]
                value = part[c, owner, :, lanes]
                if s > 1 or h == side:
                    value = value + msg_in[side, s - 1, c, :, lanes].astype(F32)
                if s < 3:
                    msg_out[side, s, c, :, lanes] = value.astype(BF16)
                elif h == side:
                    wide_out[side, c] = value
                else:
                    low_out[side, c] = value.astype(BF16)
            if s < 3:
                msg_copy(side, s, c).start()
            else:
                wide_copy(side, c).start()
                low_copy(side, c).start()

    def sum_end(c):
        for side in range(2):
            wide_copy(side, c).wait_recv()
            low_copy(side, c).wait_recv()
        gate = part[c, z, :, halves[0]] + wide_in[0, c] + low_in[1, c].astype(F32)
        up = part[c, z, :, halves[1]] + wide_in[1, c] + low_in[0, c].astype(F32)
        hid[c, z] = (gate / (1.0 + jnp.exp(-gate)) * up).astype(BF16)
        for side in range(2):
            ag_copy(side, 0, c).start()

    def gather_step(s, c):
        for side in range(2):
            ag_copy(side, s - 1, c).wait_recv()
            ag_copy(side, s, c).start()
            if s == 2:
                ag_copy(side, 3, c).start()

    def gather_end(c):
        for side in range(2):
            ag_copy(side, 2, c).wait_recv()
            ag_copy(side, 3, c).wait_recv()
        down_matmul(c)
        ex_copy(c).start()

    def send_result(c):
        ex_copy(c).wait_recv()
        for p in range(2):
            value = term[c, p, core] + sibling[c, p]
            term[c, p, core] = value
            out_send[c, p] = value.astype(BF16)
            others(c, p, lambda: res_copy(c, p).start())

    send_wave(0)
    for i in range(4):
        w_copies[2 * i].wait()
        w_copies[2 * i + 1].wait()
        mask_pair(i)
    own_copy.wait()
    for k, p, _, _ in WAVES[0]:
        tok_wait(k, p).wait_recv()
    send_wave(1)
    for k in range(2):
        fwd_copy(k).start()

    def at(slot, stage, *args):
        @pl.when(jnp.logical_and(slot >= 0, slot < SLOTS))
        def _():
            double = slot < DOUBLE
            first = jnp.where(double, 2 * slot, slot + DOUBLE)

            @pl.loop(first, first + jnp.where(double, 2, 1))
            def _(c):
                stage(*args, c)

    def bring(t, plan):
        for slot, places, chunks, wave in plan:
            @pl.when(t == slot)
            def _():
                for place in places:
                    tok_wait(*place).wait_recv()
                for k in chunks:
                    fwd_copy(k).start()
                if wave is not None:
                    send_wave(wave)

    def bring_late(t):
        bring(t, (
            (1, ((2, 0), (2, 1), (6, 0), (6, 1)), (2,), 2),
            (2, ((3, 0), (3, 1)), (3,), 3),
        ))

    def bring_early(t):
        bring(t, (
            (3, ((4, 0), (4, 1)), (4,), None),
            (4, ((5, 0), (5, 1)), (5, 6), None),
            (5, ((7, 1),), (7,), None),
        ))

    def matmul(c):
        fwd_copy(c).wait_recv()
        first_matmul(c)
        sum_start(c)

    def prepare_down(t):
        @pl.when(t == 0)
        def _():
            d_copy.wait()

        @pl.when(t < ff // BLOCK)
        def _():
            mask_down(t)

    def collect(c):
        for p in range(2):
            others(c, p, lambda: res_copy(c, p).wait_recv())

        @pl.when(c == 0)
        def _():
            acc[...] = term[0, 0, core] + out_recv[0, 1].astype(F32)

        @pl.when(c > 0)
        def _():
            acc[...] = acc[...] + (out_recv[c, 0].astype(F32) + out_recv[c, 1].astype(F32))

    stages = {
        "bring_late": bring_late,
        "bring_early": bring_early,
        "prepare_down": prepare_down,
        "matmul": lambda t: at(t, matmul),
        "sum1": lambda t: at(t - 1, sum_step, 1),
        "sum2": lambda t: at(t - 2, sum_step, 2),
        "sum3": lambda t: at(t - 3, sum_step, 3),
        "sum_end": lambda t: at(t - 4, sum_end),
        "gather1": lambda t: at(t - 5, gather_step, 1),
        "gather2": lambda t: at(t - 6, gather_step, 2),
        "gather_end": lambda t: at(t - 7, gather_end),
        "send_result": lambda t: at(t - 7, send_result),
        "collect": lambda t: at(t - 9, collect),
    }

    @pl.loop(0, SLOTS + 7)
    def _(t):
        for name in ORDER:
            stages[name](t)

    late = ((6, 0), (6, 1), (7, 0), (7, 1))
    for place in late:
        res_copy(*place).wait_recv()
    total = acc[...]
    for k, p in late:
        total = total + out_recv[k, p].astype(F32)
    out[...] = total.astype(BF16)

    @pl.loop(0, CHUNKS)
    def _(c):
        for side in range(2):
            for s in range(3):
                msg_copy(side, s, c).wait_send()
            low_copy(side, c).wait_send()
            wide_copy(side, c).wait_send()
            for s in range(4):
                ag_copy(side, s, c).wait_send()
        fwd_copy(c).wait_send()
        ex_copy(c).wait_send()

    @pl.loop(0, CHUNKS)
    def _(k):
        for p in range(2):
            others(k, p, lambda: tok_wait(k, p).wait_send())
            others(k, p, lambda: res_copy(k, p).wait_send())


def body(tokens, gate_weight, up_weight, down_weight, gate_mask, up_mask, down_mask):
    depth, ff = gate_weight.shape
    wide = down_weight.shape[1]
    own_tokens = tokens.shape[0]
    dma = pltpu.SemaphoreType.DMA
    chips = SIDE * SIDE
    smem = pl.BlockSpec(memory_space=pltpu.SMEM)
    anywhere = pl.BlockSpec(memory_space=pl.ANY)
    n_tokens = own_tokens * chips * CORES
    return pl.pallas_call(
        kernel,
        out_shape=jax.ShapeDtypeStruct((own_tokens, wide), BF16),
        in_specs=[smem] * 3 + [anywhere] * 4,
        out_specs=pl.BlockSpec(memory_space=pltpu.VMEM),
        scratch_shapes=[
            pltpu.VMEM((depth, 2 * ff), BF16),
            pltpu.VMEM((ff, wide), BF16),
            pltpu.VMEM((CHUNKS, 2, CORES, own_tokens, depth), BF16),
            pltpu.VMEM((CHUNKS, ROWS, OWN, 2 * ff), F32),
            pltpu.VMEM((2, 3, CHUNKS, OWN, 2 * ff), BF16),
            pltpu.VMEM((2, 3, CHUNKS, OWN, 2 * ff), BF16),
            pltpu.VMEM((2, CHUNKS, OWN, ff), BF16),
            pltpu.VMEM((2, CHUNKS, OWN, ff), BF16),
            pltpu.VMEM((2, CHUNKS, OWN, ff), F32),
            pltpu.VMEM((2, CHUNKS, OWN, ff), F32),
            pltpu.VMEM((CHUNKS, ROWS, OWN, ff), BF16),
            pltpu.VMEM((CHUNKS, 2, CORES, own_tokens, wide), F32),
            pltpu.VMEM((CHUNKS, 2, own_tokens, wide), F32),
            pltpu.VMEM((CHUNKS, 2, own_tokens, wide), BF16),
            pltpu.VMEM((CHUNKS, 2, own_tokens, wide), BF16),
            pltpu.VMEM((own_tokens, wide), F32),
            dma((3, 4)),
            dma,
            dma((CHUNKS, 2)), dma((CHUNKS, 2)),
            dma((CHUNKS,)), dma((CHUNKS,)),
            dma((2, 3, CHUNKS)), dma((2, 3, CHUNKS)),
            dma((2, CHUNKS)), dma((2, CHUNKS)),
            dma((2, CHUNKS)), dma((2, CHUNKS)),
            dma((2, 4, CHUNKS)), dma((2, 4, CHUNKS)),
            dma((CHUNKS,)), dma((CHUNKS,)),
            dma((CHUNKS, 2)), dma((CHUNKS, 2)),
        ],
        compiler_params=pltpu.CompilerParams(
            collective_id=0, has_side_effects=True, vmem_limit_bytes=60 * 2**20
        ),
        cost_estimate=pl.CostEstimate(
            flops=6 * n_tokens * depth * ff,
            bytes_accessed=6 * depth * ff,
            transcendentals=n_tokens * ff // ROWS,
        ),
    )(gate_mask, up_mask, down_mask, tokens, gate_weight, up_weight, down_weight)


def solution(mesh):
    placed = (
        P("col", "row"),
        P("row", "col"),
        P("row", "col"),
        P("col", "row"),
        P("row", "col"),
        P("row", "col"),
        P("col", "row"),
    )
    return jax.shard_map(
        body, mesh=mesh, in_specs=placed, out_specs=P("col", "row"), check_vma=False
    )
```

```python
import functools

import jax
import jax.numpy as jnp
from jax import lax
from jax.experimental import pallas as pl
from jax.experimental.pallas import tpu as pltpu
from jax.sharding import PartitionSpec as P

MESH = pl.DeviceIdType.MESH
BLOCK = 128
ROWS = 8
SIDE = 4
CORES = 2
CHUNKS = 8
OWN = 16
WIDTH1 = 896
WIDTH2 = 1024
GROUP = 1
AHEAD = 2
OFFSETS = (
    ((0, 0), (1, 0)),
    ((3, 0), (0, 1)),
    ((1, 1), (0, 2)),
    ((2, 1), (1, 2)),
    ((3, 2), (2, 3)),
    ((2, 2), (3, 3)),
    ((3, 1), (1, 3)),
    ((0, 3), (2, 0)),
)
OWN_PLACE = (0, 0)
WAVES = (
    (
        (0, 1, (1, 0), OWN_PLACE),
        (1, 0, (-1, 0), OWN_PLACE),
        (1, 1, (0, 1), OWN_PLACE),
        (7, 0, (0, -1), OWN_PLACE),
    ),
    (
        (2, 0, (0, 1), (0, 1)),
        (2, 1, (0, -1), (7, 0)),
        (6, 1, (1, 0), (7, 0)),
        (6, 0, (-1, 0), (1, 1)),
    ),
    (
        (3, 0, (1, 0), (2, 0)),
        (3, 1, (0, 1), (2, 0)),
        (4, 0, (-1, 0), (2, 1)),
        (4, 1, (1, 0), (6, 1)),
    ),
    (
        (5, 0, (1, 0), (3, 1)),
        (5, 1, (0, -1), (1, 0)),
        (7, 1, (-1, 0), (1, 0)),
    ),
)
DOUBLE = 1
SLOTS = CHUNKS - DOUBLE
ORDER = (
    "bring_early",
    "gather2",
    "gather1",
    "prepare_down",
    "gather_end",
    "sum_end",
    "sum3",
    "send_result",
    "sum2",
    "sum1",
    "bring_late",
    "matmul",
    "collect",
)
DX, DY = (
    tuple(sum(pair[p][i] * 4**k for k, pair in enumerate(OFFSETS)) for p in range(2))
    for i in range(2)
)


def pick(digits, k):
    return lax.rem(lax.shift_right_logical(jnp.int32(digits), jnp.int32(2 * k)), 4)

BF16 = jnp.bfloat16
F32 = jnp.float32


def kernel(
    gate_mask, up_mask, down_mask, tokens, gate_weight, up_weight, down_weight, out,
    pair, down, tok, part, msg_out, msg_in, low_out, low_in, wide_out, wide_in,
    hid, term, sibling, out_send, out_recv, acc,
    w_sem, tok_own, tok_send, tok_recv, fwd_send, fwd_recv,
    msg_send, msg_recv, low_send, low_recv, wide_send, wide_recv,
    ag_send, ag_recv, ex_send, ex_recv, res_send, res_recv,
):
    z = lax.axis_index("row")
    col = lax.axis_index("col")
    core = lax.rem(col, CORES)
    chip = lax.div(col, CORES)
    x = lax.rem(chip, SIDE)
    y = lax.div(chip, SIDE)
    ff = gate_weight.shape[1]
    depth = gate_weight.shape[0]
    halves = (slice(0, ff), slice(ff, 2 * ff))

    def ring(step):
        return lax.rem(z + step + ROWS, ROWS)

    def at_offset(k, p, sign, to_core):
        dx, dy = pick(DX[p], k), pick(DY[p], k)
        x2 = lax.rem(x + sign * dx + SIDE, SIDE)
        y2 = lax.rem(y + sign * dy + SIDE, SIDE)
        return (z, (y2 * SIDE + x2) * CORES + to_core)

    def remote(src, dst, send, recv, device):
        return pltpu.make_async_remote_copy(
            src_ref=src, dst_ref=dst, send_sem=send, recv_sem=recv,
            device_id=device, device_id_type=MESH,
        )

    mate = (z, chip * CORES + 1 - core)
    neighbour = ((ring(1), col), (ring(-1), col))
    second = ((ring(2), col), (ring(-2), col))

    quarter = depth // 4
    w_copies = []
    for i in range(4):
        rows = slice(i * quarter, (i + 1) * quarter)
        for h, w in enumerate((gate_weight, up_weight)):
            w_copies.append(
                pltpu.make_async_copy(w.at[rows], pair.at[rows, halves[h]], w_sem.at[h, i])
            )
    d_copy = pltpu.make_async_copy(down_weight, down, w_sem.at[2, 0])
    own_copy = pltpu.make_async_copy(tokens, tok.at[OWN_PLACE[0], OWN_PLACE[1], core], tok_own)
    own_copy.start()
    for copy in w_copies:
        copy.start()
    d_copy.start()

    barrier = pltpu.get_barrier_semaphore()
    pl.semaphore_signal(barrier, inc=1, device_id=mate, device_id_type=MESH)
    for side in range(2):
        pl.semaphore_signal(barrier, inc=1, device_id=neighbour[side], device_id_type=MESH)
        pl.semaphore_signal(barrier, inc=1, device_id=second[side], device_id_type=MESH)

    def others(k, p, run):
        if p == 1:
            run()
        else:
            pl.when(k > 0)(run)

    @pl.loop(0, CHUNKS)
    def _(k):
        for p in range(2):
            others(k, p, lambda: pl.semaphore_signal(
                barrier, inc=1, device_id=at_offset(k, p, 1, core), device_id_type=MESH
            ))

    pl.semaphore_wait(barrier, SIDE * SIDE - 1 + 5)

    def send_wave(number):
        for k, p, (dx, dy), (from_k, from_p) in WAVES[number]:
            x2, y2 = lax.rem(x - dx + SIDE, SIDE), lax.rem(y - dy + SIDE, SIDE)
            src = tokens if number == 0 else tok.at[from_k, from_p, core]
            remote(
                src, tok.at[k, p, core], tok_send.at[k, p], tok_recv.at[k, p],
                (z, (y2 * SIDE + x2) * CORES + core),
            ).start()

    def tok_wait(k, p):
        return remote(
            tok.at[k, p, core], tok.at[k, p, core], tok_send.at[k, p], tok_recv.at[k, p], mate
        )

    def fwd_copy(k):
        return remote(tok.at[k, :, core], tok.at[k, :, core], fwd_send.at[k], fwd_recv.at[k], mate)

    def msg_copy(side, s, c):
        src, dst = msg_out.at[side, s, c], msg_in.at[side, s, c]
        if s == 0:
            src, dst = src.at[:, halves[side]], dst.at[:, halves[side]]
        return remote(src, dst, msg_send.at[side, s, c], msg_recv.at[side, s, c], neighbour[side])

    def low_copy(side, c):
        return remote(
            low_out.at[side, c], low_in.at[side, c],
            low_send.at[side, c], low_recv.at[side, c], neighbour[side],
        )

    def wide_copy(side, c):
        return remote(
            wide_out.at[side, c], wide_in.at[side, c],
            wide_send.at[side, c], wide_recv.at[side, c], neighbour[side],
        )

    cut = 4 * BLOCK

    def ag_ref(side, s, c, owner):
        ref = hid.at[c, owner]
        if s == 3:
            ref = ref.at[:, slice(0, cut) if side == 0 else slice(cut, ff)]
        return ref

    def ag_copy(side, s, c):
        far = min(s, 2)
        block = ag_ref(side, s, c, ring(-far if side == 0 else far))
        device = second[side] if s == 3 else neighbour[side]
        return remote(block, block, ag_send.at[side, s, c], ag_recv.at[side, s, c], device)

    parts = tuple(slice(h * WIDTH2, (h + 1) * WIDTH2) for h in range(down.shape[1] // WIDTH2))

    def ex_copy(c, h):
        return remote(
            term.at[c, :, 1 - core, :, parts[h]], sibling.at[c, :, :, parts[h]],
            ex_send.at[c, h], ex_recv.at[c, h], mate,
        )

    def res_copy(k, p, h):
        return remote(
            out_send.at[k, p, :, parts[h]], out_recv.at[k, p, :, parts[h]],
            res_send.at[k, p, h], res_recv.at[k, p, h], at_offset(k, p, 1, core),
        )

    def each_part(run):
        for h in range(len(parts)):
            run(h)

    def keep(ref, rows, lanes, flag):
        scale = jnp.full((BLOCK, BLOCK), flag.astype(F32), F32).astype(BF16)
        ref[rows, lanes] = ref[rows, lanes] * scale

    def mask_pair(i):
        @pl.loop(0, quarter // BLOCK)
        def _(r):
            block = i * (quarter // BLOCK) + r
            rows = pl.ds(pl.multiple_of(block * BLOCK, BLOCK), BLOCK)
            for h, mask in enumerate((gate_mask, up_mask)):
                for b in range(ff // BLOCK):
                    start = h * ff + b * BLOCK
                    keep(pair, rows, slice(start, start + BLOCK), mask[block, b])

    def mask_down(r):
        rows = pl.ds(pl.multiple_of(r * BLOCK, BLOCK), BLOCK)
        for b in range(down.shape[1] // BLOCK):
            keep(down, rows, slice(b * BLOCK, (b + 1) * BLOCK), down_mask[r, b])

    def first_matmul(c):
        @pl.loop(0, 2 * ff // WIDTH1)
        def _(n):
            lanes = pl.ds(pl.multiple_of(n * WIDTH1, WIDTH1), WIDTH1)
            value = jnp.dot(
                tok[pl.ds(c, GROUP)].reshape(GROUP * ROWS * OWN, depth),
                pair[:, lanes],
                preferred_element_type=F32,
            )
            part[pl.ds(c, GROUP), :, :, lanes] = value.reshape(GROUP, ROWS, OWN, WIDTH1)

    def down_matmul(c):
        for h, lanes in enumerate(parts):
            value = jnp.dot(
                hid[c].reshape(ROWS * OWN, ff), down[:, lanes], preferred_element_type=F32
            )
            term[c, :, :, :, lanes] = value.reshape(2, CORES, 2 * OWN, WIDTH2)
            ex_copy(c, h).start()

    def sum_start(c):
        owner = ring(4)
        for side in range(2):
            h = halves[side]
            msg_out[side, 0, c, :, h] = part[c, owner, :, h].astype(BF16)
            msg_copy(side, 0, c).start()

    def sum_step(s, c):
        for side in range(2):
            owner = ring(4 - s if side == 0 else s - 4)
            msg_copy(side, s - 1, c).wait_recv()
            for h in range(2):
                lanes = halves[h]
                value = part[c, owner, :, lanes]
                if s > 1 or h == side:
                    value = value + msg_in[side, s - 1, c, :, lanes].astype(F32)
                if s < 3:
                    msg_out[side, s, c, :, lanes] = value.astype(BF16)
                elif h == side:
                    wide_out[side, c] = value
                else:
                    low_out[side, c] = value.astype(BF16)
            if s < 3:
                msg_copy(side, s, c).start()
            else:
                wide_copy(side, c).start()
                low_copy(side, c).start()

    def sum_end(c):
        for side in range(2):
            wide_copy(side, c).wait_recv()
            low_copy(side, c).wait_recv()
        gate = part[c, z, :, halves[0]] + wide_in[0, c] + low_in[1, c].astype(F32)
        up = part[c, z, :, halves[1]] + wide_in[1, c] + low_in[0, c].astype(F32)
        hid[c, z] = (gate / (1.0 + jnp.exp(-gate)) * up).astype(BF16)
        for side in range(2):
            ag_copy(side, 0, c).start()

    def gather_step(s, c):
        for side in range(2):
            ag_copy(side, s - 1, c).wait_recv()
            ag_copy(side, s, c).start()
            if s == 2:
                ag_copy(side, 3, c).start()

    def gather_end(c):
        for side in range(2):
            ag_copy(side, 2, c).wait_recv()
            ag_copy(side, 3, c).wait_recv()
        down_matmul(c)

    def send_result(c):
        for h, lanes in enumerate(parts):
            ex_copy(c, h).wait_recv()
            for p in range(2):
                value = term[c, p, core, :, lanes] + sibling[c, p, :, lanes]
                term[c, p, core, :, lanes] = value
                out_send[c, p, :, lanes] = value.astype(BF16)
                others(c, p, lambda: res_copy(c, p, h).start())

    send_wave(0)
    for i in range(4):
        w_copies[2 * i].wait()
        w_copies[2 * i + 1].wait()
        mask_pair(i)
    own_copy.wait()
    for k, p, _, _ in WAVES[0]:
        tok_wait(k, p).wait_recv()
    send_wave(1)
    for k in range(2):
        fwd_copy(k).start()

    def at(slot, stage, *args):
        @pl.when(jnp.logical_and(slot >= 0, slot < SLOTS))
        def _():
            double = slot < DOUBLE
            first = jnp.where(double, 2 * slot, slot + DOUBLE)

            @pl.loop(first, first + jnp.where(double, 2, 1))
            def _(c):
                stage(*args, c)

    def bring(t, plan):
        for slot, places, chunks, wave in plan:
            @pl.when(t == slot)
            def _():
                for place in places:
                    tok_wait(*place).wait_recv()
                for k in chunks:
                    fwd_copy(k).start()
                if wave is not None:
                    send_wave(wave)

    def bring_late(t):
        bring(t, (
            (1, ((2, 0), (2, 1), (6, 0), (6, 1)), (2,), 2),
            (2, ((3, 0), (3, 1)), (3,), 3),
        ))

    def bring_early(t):
        bring(t, (
            (3, ((4, 0), (4, 1)), (4,), None),
            (4, ((5, 0), (5, 1)), (5, 6), None),
            (5, ((7, 1),), (7,), None),
        ))

    def matmul(c):
        fwd_copy(c).wait_recv()
        first_matmul(c)
        sum_start(c)

    def prepare_down(t):
        @pl.when(t == 0)
        def _():
            d_copy.wait()

        @pl.when(t < ff // BLOCK)
        def _():
            mask_down(t)

    def collect(c):
        for p in range(2):
            others(c, p, lambda: each_part(lambda h: res_copy(c, p, h).wait_recv()))

        @pl.when(c == 0)
        def _():
            acc[...] = term[0, 0, core] + out_recv[0, 1].astype(F32)

        @pl.when(c > 0)
        def _():
            acc[...] = acc[...] + (out_recv[c, 0].astype(F32) + out_recv[c, 1].astype(F32))

    stages = {
        "bring_late": bring_late,
        "bring_early": bring_early,
        "prepare_down": prepare_down,
        "matmul": lambda t: at(t, matmul),
        "sum1": lambda t: at(t - 1, sum_step, 1),
        "sum2": lambda t: at(t - 2, sum_step, 2),
        "sum3": lambda t: at(t - 3, sum_step, 3),
        "sum_end": lambda t: at(t - 4, sum_end),
        "gather1": lambda t: at(t - 5, gather_step, 1),
        "gather2": lambda t: at(t - 6, gather_step, 2),
        "gather_end": lambda t: at(t - 7, gather_end),
        "send_result": lambda t: at(t - 7, send_result),
        "collect": lambda t: at(t - 9, collect),
    }

    @pl.loop(0, SLOTS + 7)
    def _(t):
        for name in ORDER:
            stages[name](t)

    late = ((6, 0), (6, 1), (7, 0), (7, 1))
    for h, lanes in enumerate(parts):
        total = acc[:, lanes]
        for k, p in late:
            res_copy(k, p, h).wait_recv()
            total = total + out_recv[k, p, :, lanes].astype(F32)
        out[:, lanes] = total.astype(BF16)

    @pl.loop(0, CHUNKS)
    def _(c):
        for side in range(2):
            for s in range(3):
                msg_copy(side, s, c).wait_send()
            low_copy(side, c).wait_send()
            wide_copy(side, c).wait_send()
            for s in range(4):
                ag_copy(side, s, c).wait_send()
        fwd_copy(c).wait_send()
        each_part(lambda h: ex_copy(c, h).wait_send())

    @pl.loop(0, CHUNKS)
    def _(k):
        for p in range(2):
            others(k, p, lambda: tok_wait(k, p).wait_send())
            others(k, p, lambda: each_part(lambda h: res_copy(k, p, h).wait_send()))


def body(tokens, gate_weight, up_weight, down_weight, gate_mask, up_mask, down_mask):
    depth, ff = gate_weight.shape
    wide = down_weight.shape[1]
    own_tokens = tokens.shape[0]
    dma = pltpu.SemaphoreType.DMA
    chips = SIDE * SIDE
    smem = pl.BlockSpec(memory_space=pltpu.SMEM)
    anywhere = pl.BlockSpec(memory_space=pl.ANY)
    n_tokens = own_tokens * chips * CORES
    return pl.pallas_call(
        kernel,
        out_shape=jax.ShapeDtypeStruct((own_tokens, wide), BF16),
        in_specs=[smem] * 3 + [anywhere] * 4,
        out_specs=pl.BlockSpec(memory_space=pltpu.VMEM),
        scratch_shapes=[
            pltpu.VMEM((depth, 2 * ff), BF16),
            pltpu.VMEM((ff, wide), BF16),
            pltpu.VMEM((CHUNKS, 2, CORES, own_tokens, depth), BF16),
            pltpu.VMEM((CHUNKS, ROWS, OWN, 2 * ff), F32),
            pltpu.VMEM((2, 3, CHUNKS, OWN, 2 * ff), BF16),
            pltpu.VMEM((2, 3, CHUNKS, OWN, 2 * ff), BF16),
            pltpu.VMEM((2, CHUNKS, OWN, ff), BF16),
            pltpu.VMEM((2, CHUNKS, OWN, ff), BF16),
            pltpu.VMEM((2, CHUNKS, OWN, ff), F32),
            pltpu.VMEM((2, CHUNKS, OWN, ff), F32),
            pltpu.VMEM((CHUNKS, ROWS, OWN, ff), BF16),
            pltpu.VMEM((CHUNKS, 2, CORES, own_tokens, wide), F32),
            pltpu.VMEM((CHUNKS, 2, own_tokens, wide), F32),
            pltpu.VMEM((CHUNKS, 2, own_tokens, wide), BF16),
            pltpu.VMEM((CHUNKS, 2, own_tokens, wide), BF16),
            pltpu.VMEM((own_tokens, wide), F32),
            dma((3, 4)),
            dma,
            dma((CHUNKS, 2)), dma((CHUNKS, 2)),
            dma((CHUNKS,)), dma((CHUNKS,)),
            dma((2, 3, CHUNKS)), dma((2, 3, CHUNKS)),
            dma((2, CHUNKS)), dma((2, CHUNKS)),
            dma((2, CHUNKS)), dma((2, CHUNKS)),
            dma((2, 4, CHUNKS)), dma((2, 4, CHUNKS)),
            dma((CHUNKS, 2)), dma((CHUNKS, 2)),
            dma((CHUNKS, 2, 2)), dma((CHUNKS, 2, 2)),
        ],
        compiler_params=pltpu.CompilerParams(
            collective_id=0, has_side_effects=True, vmem_limit_bytes=60 * 2**20
        ),
        cost_estimate=pl.CostEstimate(
            flops=6 * n_tokens * depth * ff,
            bytes_accessed=6 * depth * ff,
            transcendentals=n_tokens * ff // ROWS,
        ),
    )(gate_mask, up_mask, down_mask, tokens, gate_weight, up_weight, down_weight)


def solution(mesh):
    placed = (
        P("col", "row"),
        P("row", "col"),
        P("row", "col"),
        P("col", "row"),
        P("row", "col"),
        P("row", "col"),
        P("col", "row"),
    )
    return jax.shard_map(
        body, mesh=mesh, in_specs=placed, out_specs=P("col", "row"), check_vma=False
    )
```
